32 devices in a mesh: section: 2 (over core), dp: 16 (over z, y, x).
Axes of the slice: x: 2, y: 2, z: 4, core: 2. Of those that a mesh axis runs over, the one named last changes fastest.
Arguments:
- tokens: bfloat16 [8192, 1024], P('dp'), may hold values from -6 to 6
- cotangent: bfloat16 [8192, 1024], P('dp'), may hold values from -6 to 6
- lengths: int32 [16, 2, 4], P('dp'), may hold values from 1 to 128, 256 in all within a row
- w_in: bfloat16 [2, 1024, 3352], P('section'), may hold values from -0.1875 to 0.1875
- conv_w: float32 [2, 4, 1792], P('section'), may hold values from -4 to 4
- conv_b: float32 [2, 1792], P('section'), may hold values from -3 to 3
- dt_bias: float32 [2, 24], P('section'), may hold values from -3 to 0.5
- a_log: float32 [2, 24], P('section'), may hold values from -3 to 1
- d_skip: float32 [2, 24], P('section'), may hold values from 0.3 to 1.5
- g_mix: float32 [2, 1024], P('section'), may hold values from 0.25 to 1.75
- g_ssm: float32 [2, 1536], P('section'), may hold values from 0.25 to 1.75
- w_out: bfloat16 [2, 1536, 1024], P('section'), may hold values from -0.15625 to 0.15625
- w_qkv: bfloat16 [2, 1024, 768], P('section'), may hold values from -0.1875 to 0.1875
- w_o: bfloat16 [2, 512, 1024], P('section'), may hold values from -0.75 to 0.75
- g_ffn: float32 [2, 1024], P('section'), may hold values from 0.25 to 1.75
- w_gu: bfloat16 [2, 1024, 4096], P('section'), may hold values from -0.1875 to 0.1875
- w_down: bfloat16 [2, 2048, 1024], P('section'), may hold values from -0.125 to 0.125
Outputs:
- layer_out: bfloat16 [2, 8192, 1024], P('section', 'dp')
- input_grad: bfloat16 [2, 8192, 1024], P('section', 'dp')
- grad_w_in: float32 [2, 1024, 3352], P('section', 'dp')
- grad_conv_w: float32 [2, 4, 1792], P('section')
- grad_conv_b: float32 [2, 1792], P('section')
- grad_dt_bias: float32 [2, 24], P('section')
- grad_a_log: float32 [2, 24], P('section')
- grad_d_skip: float32 [2, 24], P('section')
- grad_g_mix: float32 [2, 1024], P('section', 'dp')
- grad_g_ssm: float32 [2, 1536], P('section', 'dp')
- grad_w_out: float32 [2, 1536, 1024], P('section', 'dp')
- grad_w_qkv: float32 [2, 1024, 768], P('section', 'dp')
- grad_w_o: float32 [2, 512, 1024], P('section', 'dp')
- grad_g_ffn: float32 [2, 1024], P('section', 'dp')
- grad_w_gu: float32 [2, 1024, 4096], P('section', 'dp')
- grad_w_down: float32 [2, 2048, 1024], P('section', 'dp')
The draws below stay inside these ranges and needn't reach their ends.
Inputs may be any that keep to these rules, and one draw needn't show every extreme that they name: `lengths`: each row sums to 256; the longest sequence of each micro-batch has 128 tokens.
All inputs are finite; a program needn't handle non-finite values.
Results may differ from the reference program's by a relative error of at most 0.028.
Values may be sent and summed in bfloat16 or wider, within the bound.
A program may use at most 320 MiB of HBM per device.

```python
import math
import jax
import jax.numpy as jnp
import numpy as np
from jax import lax

D = 1024
NH = 24
MH = 64
NS = 128
QH = 8
KVH = 2
AH = 64
FF = 2048
CONV = 4
MICRO = 2
SEQS = 4
MB_TOK = 256
LONGEST = 128
DI = 1536
TOKENS = 8192
N_DP = 16


def steps_of(rng, extent, split, smallest, top_value):
    def one(dim, parts):
        heights = jax.random.uniform(jax.random.fold_in(jax.random.fold_in(rng, 6), dim), (parts,), jnp.float32, smallest / len(split), top_value / len(split))
        return jnp.repeat(jnp.exp(heights), extent[dim] // parts).reshape((-1,) + (1,) * (len(extent) - dim - 1))

    level = one(*split[0])
    for cut in split[1:]:
        level = level * one(*cut)
    return level


def split_up(number_of, total, limit, lean):
    weights = [(1 << 20) // math.isqrt(standing ** lean) + 1 for standing in range(2, number_of + 1)]
    surplus, given = total - limit - (number_of - 1), [1] * (number_of - 1)
    while surplus > 0:
        movable = [i for i in range(number_of - 1) if given[i] < limit]
        mass, left = sum([weights[i] for i in movable]), surplus
        for i in movable:
            more = min(limit - given[i], max(1, left * weights[i] // mass), surplus)
            given[i] = given[i] + more
            surplus = surplus - more
    return np.array([limit] + given)


def uneven(key, amount, total, bound, lean):
    if amount == 2:
        one = jax.random.randint(key, (), max(1, total - bound), min(bound, total - 1) + 1)
        return jnp.stack([one, total - one])
    tallies = jnp.asarray(split_up(amount, total, bound, lean), jnp.int32)
    twos = (amount - 1) // 2
    source_of, sink = tallies[1:1 + 2 * twos:2], tallies[2:2 + 2 * twos:2]
    room = jnp.minimum(source_of - 1, bound - sink)
    shifted = jax.random.randint(jax.random.fold_in(key, 1), (twos,), 0, 1 << 20) % (room + 1)
    tallies = tallies.at[1:1 + 2 * twos:2].set(source_of - shifted).at[2:2 + 2 * twos:2].set(sink + shifted)
    return tallies[jax.random.permutation(jax.random.fold_in(key, 2), amount)]


def normal_values(own_key, shape, scale, limit, shards=(), kind=jnp.bfloat16):
    level = steps_of(own_key, shape, shards, -0.22, 0.18) if shards else 1.0
    array = jax.random.normal(own_key, shape, jnp.float32) * scale * level
    return jnp.minimum(jnp.maximum(array, -limit), limit).astype(kind)


def setup_inputs(seed: int = 0) -> dict:
    arg_keys = jax.random.split(jax.random.key(seed), 18)
    tokens = normal_values(arg_keys[0], (TOKENS, D), 1.0, 6.0, ((0, 16),))
    cotangent = normal_values(arg_keys[1], (TOKENS, D), 1.0, 6.0, ((0, 16),))
    lengths = jax.vmap(lambda own: uneven(own, SEQS, MB_TOK, LONGEST, 2))(jax.random.split(arg_keys[2], N_DP * MICRO)).reshape((N_DP, MICRO, SEQS)).astype(jnp.int32)
    w_in = normal_values(arg_keys[3], (2, D, 2 * DI + 2 * NS + NH), D ** -0.5, 0.1875, ((0, 2),))
    conv_w = normal_values(arg_keys[4], (2, CONV, DI + 2 * NS), 2 ** -0.5, 4.0, ((0, 2),), jnp.float32)
    conv_b = normal_values(arg_keys[5], (2, DI + 2 * NS), 0.5, 3.0, ((0, 2),), jnp.float32)
    dt_bias = jnp.clip(-3.0 + 3.5 * jax.random.uniform(arg_keys[6], (2, NH), jnp.float32) ** steps_of(arg_keys[6], (2, NH), ((0, 2),), -0.2, 0.2), -3.0, 0.5)
    a_log = jnp.clip(-3.0 + 4.0 * jax.random.uniform(arg_keys[7], (2, NH), jnp.float32) ** steps_of(arg_keys[7], (2, NH), ((0, 2),), -0.2, 0.2), -3.0, 1.0)
    d_skip = jnp.clip(0.3 + 1.2 * jax.random.uniform(arg_keys[8], (2, NH), jnp.float32) ** steps_of(arg_keys[8], (2, NH), ((0, 2),), -0.2, 0.2), 0.3, 1.5)
    g_mix = jnp.clip(1.0 + 0.15 * jax.random.normal(arg_keys[9], (2, D), jnp.float32), 0.25, 1.75)
    g_ssm = jnp.clip(1.0 + 0.15 * jax.random.normal(arg_keys[10], (2, DI), jnp.float32), 0.25, 1.75)
    w_out = normal_values(arg_keys[11], (2, DI, D), DI ** -0.5, 0.15625, ((0, 2),))
    w_qkv = normal_values(arg_keys[12], (2, D, (QH + 2 * KVH) * AH), D ** -0.5, 0.1875, ((0, 2),))
    w_o = normal_values(arg_keys[13], (2, QH * AH, D), (QH * AH // 8) ** -0.5, 0.75, ((0, 2),))
    g_ffn = jnp.clip(1.0 + 0.15 * jax.random.normal(arg_keys[14], (2, D), jnp.float32), 0.25, 1.75)
    w_gu = normal_values(arg_keys[15], (2, D, 2 * FF), D ** -0.5, 0.1875, ((0, 2),))
    w_down = normal_values(arg_keys[16], (2, FF, D), FF ** -0.5, 0.125, ((0, 2),))
    return dict(tokens=tokens, cotangent=cotangent, lengths=lengths, w_in=w_in, conv_w=conv_w, conv_b=conv_b, dt_bias=dt_bias, a_log=a_log, d_skip=d_skip, g_mix=g_mix, g_ssm=g_ssm, w_out=w_out, w_qkv=w_qkv, w_o=w_o, g_ffn=g_ffn, w_gu=w_gu, w_down=w_down)


@jax.custom_vjp
def low(v):
    return lax.optimization_barrier(v.astype(jnp.bfloat16)).astype(jnp.float32)

@jax.custom_vjp
def low_back(v):
    return v

def low_keep(v):
    return (low(v), None)

def low_pass(kept, grad):
    return (grad,)

def back_keep(v):
    return (v, None)

def back_low(kept, grad):
    return (low(grad),)
low.defvjp(low_keep, low_pass)
low_back.defvjp(back_keep, back_low)
epsilon = 1e-05
ROPE_BASE = 10000.0

def product(left, right):
    return jnp.dot(left, right, precision=lax.Precision.HIGHEST)

def rms_norm(values, gain):
    return values * lax.rsqrt(lax.optimization_barrier(jnp.mean(values * values, axis=-1, keepdims=True)) + epsilon) * gain

def rotate(values, position):
    half = values.shape[-1] // 2
    freq = ROPE_BASE ** (-jnp.arange(half).astype(jnp.float32) / half)
    angle = position[:, None] * freq[None, :]
    cosine = jnp.cos(angle)[:, None, :]
    sine = jnp.sin(angle)[:, None, :]
    first = values[..., :half]
    second = values[..., half:]
    return jnp.concatenate([first * cosine - second * sine, second * cosine + first * sine], -1)

def segments(row):
    ends = jnp.cumsum(row)
    place = jnp.arange(MB_TOK).astype(jnp.int32)
    return lax.optimization_barrier(jnp.sum((place[:, None] >= ends[None, :]).astype(jnp.int32), axis=1)).astype(jnp.int32)

def layer(x, doc_ids, params):
    w_in, conv_w, conv_b, dt_bias, a_log, d_skip, g_mix, g_ssm, w_out, w_qkv, w_o, g_ffn, w_gu, w_down = params
    x = low_back(x)
    count = x.shape[0]
    place = jnp.arange(count).astype(jnp.int32)
    visible = (doc_ids[:, None] == doc_ids[None, :]) & (place[:, None] >= place[None, :])
    position = lax.optimization_barrier(jnp.sum(visible.astype(jnp.int32), axis=1)) - 1
    normed = low(rms_norm(x, g_mix))
    projected = product(normed, w_in)
    gate_z = projected[:, :DI]
    conv_in = projected[:, DI:2 * DI + 2 * NS]
    step_raw = projected[:, 2 * DI + 2 * NS:]
    conv = conv_b[None, :] + conv_w[0][None, :] * conv_in
    for lag in range(1, CONV):
        moved = jnp.concatenate([jnp.zeros((lag, conv_in.shape[1]), conv_in.dtype), conv_in[:count - lag]], 0)
        keep_rows = (position >= lag).astype(conv_in.dtype)
        conv = conv + conv_w[lag][None, :] * moved * keep_rows[:, None]
    conv = jax.nn.silu(conv)
    ssm_in = conv[:, :DI].reshape(count, NH, MH)
    b_proj = conv[:, DI:DI + NS]
    c_proj = conv[:, DI + NS:]
    step_size = jax.nn.softplus(step_raw + dt_bias[None, :])
    decay_sum = jnp.cumsum(step_size * (-jnp.exp(a_log))[None, :], axis=0)
    cb_scores = product(c_proj, b_proj.T)
    inside = visible[:, :, None]
    log_gap = jnp.where(inside, decay_sum[:, None, :] - decay_sum[None, :, :], 0.0)
    mix_weight = jnp.where(inside, jnp.exp(log_gap), 0.0) * cb_scores[:, :, None] * step_size[None, :, :]
    ssm_out = jnp.einsum('tsh,shp->thp', mix_weight, ssm_in, precision=lax.Precision.HIGHEST)
    ssm_out = ssm_out + d_skip[None, :, None] * ssm_in
    ssm_out = ssm_out.reshape(count, DI) * jax.nn.silu(gate_z)
    mixer = product(low(rms_norm(ssm_out, g_ssm)), w_out)
    qkv = product(normed, w_qkv)
    angle_pos = position.astype(jnp.float32)
    query = rotate(qkv[:, :QH * AH].reshape(count, QH, AH), angle_pos).reshape(count, KVH, QH // KVH, AH)
    key = rotate(qkv[:, QH * AH:(QH + KVH) * AH].reshape(count, KVH, AH), angle_pos)
    value = qkv[:, (QH + KVH) * AH:].reshape(count, KVH, AH)
    query = low(query)
    key = low(key)
    value = low(value)
    scores = jnp.einsum('tgqa,sga->gqts', query, key, precision=lax.Precision.HIGHEST) * AH ** (-0.5)
    scores = jnp.where(visible[None, None], scores, -1e+30)
    probs = low(jax.nn.softmax(scores, axis=-1))
    context = jnp.einsum('gqts,sga->tgqa', probs, value, precision=lax.Precision.HIGHEST).reshape(count, QH * AH)
    attended = product(low(context), w_o)
    middle = x + mixer + attended
    ffn_in = low(rms_norm(middle, g_ffn))
    both = product(ffn_in, w_gu)
    action = low(jax.nn.silu(both[:, :FF]) * both[:, FF:])
    return low(middle + product(action, w_down))

def reference(tokens, cotangent, lengths, w_in, conv_w, conv_b, dt_bias, a_log, d_skip, g_mix, g_ssm, w_out, w_qkv, w_o, g_ffn, w_gu, w_down):
    blocks = N_DP * MICRO
    doc_ids = jax.vmap(segments)(lengths.reshape(blocks, SEQS))
    weights = (w_in, conv_w, conv_b, dt_bias, a_log, d_skip, g_mix, g_ssm, w_out, w_qkv, w_o, g_ffn, w_gu, w_down)

    def params_of(index):
        return tuple((w[index].astype(jnp.float32) for w in weights))

    def run(inputs, params):

        def single(pair):
            return layer(pair[0], pair[1], params)
        return lax.map(jax.checkpoint(single), (inputs, doc_ids))
    first_in = tokens.astype(jnp.float32).reshape(blocks, MB_TOK, D)
    middle, back_first = jax.vjp(run, first_in, params_of(0))
    final, back_second = jax.vjp(run, middle, params_of(1))
    grad_middle, grads_second = back_second(cotangent.astype(jnp.float32).reshape(blocks, MB_TOK, D))
    grad_first, grads_first = back_first(grad_middle)
    layer_out = jnp.stack([middle.reshape(-1, D), final.reshape(-1, D)]).astype(jnp.bfloat16)
    input_grad = jnp.stack([grad_first.reshape(-1, D), grad_middle.reshape(-1, D)]).astype(jnp.bfloat16)
    stacked = [jnp.stack([a, b]) for a, b in zip(grads_first, grads_second)]
    return (layer_out, input_grad, stacked[0], stacked[1], stacked[2], stacked[3], stacked[4], stacked[5], stacked[6], stacked[7], stacked[8], stacked[9], stacked[10], stacked[11], stacked[12], stacked[13])
```

```python
import jax
import jax.numpy as jnp
from jax import lax
from jax.sharding import PartitionSpec as P

D = 1024
NH = 24
MH = 64
NS = 128
QH = 8
KVH = 2
AH = 64
FF = 2048
CONV = 4
MICRO = 2
MB_TOK = 256
DI = 1536


epsilon = 1e-05
ROPE_BASE = 10000.0


def passed_along(block, axis, distance):
    devices = range(lax.axis_size(axis))
    route = [(i - distance, i) for i in devices if i - distance in devices]
    return lax.ppermute(block, axis, route)


@jax.custom_vjp
def round_value(values):
    return values.astype(jnp.bfloat16).astype(jnp.float32)


round_value.defvjp(lambda values: (round_value(values), None), lambda kept, grad: (grad,))


def round_plain(values):
    return values.astype(jnp.bfloat16).astype(jnp.float32)


@jax.custom_vjp
def tapped(values, probe):
    return values


tapped.defvjp(lambda values, probe: (values, None), lambda kept, grad: (grad, grad))


@jax.custom_vjp
def product(left, weight):
    return jnp.dot(left.astype(jnp.bfloat16), weight, preferred_element_type=jnp.float32)


def product_back(weight, grad):
    back = lax.dot_general(
        grad.astype(jnp.bfloat16),
        weight,
        (((1,), (1,)), ((), ())),
        preferred_element_type=jnp.float32,
    )
    return back, jnp.zeros_like(weight)


product.defvjp(lambda left, weight: (product(left, weight), weight), product_back)


def contract(spec, left, right):
    return jnp.einsum(spec, left, right, precision=lax.Precision.DEFAULT)


def rms_norm(values, gain):
    return values * lax.rsqrt(jnp.mean(values * values, axis=-1, keepdims=True) + epsilon) * gain


def rotate(values, position):
    half = values.shape[-1] // 2
    freq = ROPE_BASE ** (-jnp.arange(half).astype(jnp.float32) / half)
    angle = position[:, None] * freq[None, :]
    cosine = jnp.cos(angle)[:, None, :]
    sine = jnp.sin(angle)[:, None, :]
    first = values[..., :half]
    second = values[..., half:]
    return jnp.concatenate([first * cosine - second * sine, second * cosine + first * sine], -1)


def segments(row):
    ends = jnp.cumsum(row)
    place = jnp.arange(MB_TOK)
    return jnp.sum((place[:, None] >= ends[None, :]).astype(jnp.int32), axis=1)


def layer(x, small, probes, doc_ids, large):
    conv_w, conv_b, dt_bias, a_log, d_skip, g_mix, g_ssm, g_ffn = small
    w_in, w_out, w_qkv, w_o, w_gu, w_down = large
    count = x.shape[0]
    place = jnp.arange(count)
    earlier = place[:, None] >= place[None, :]
    visible = (doc_ids[:, None] == doc_ids[None, :]) & earlier
    position = jnp.sum(visible.astype(jnp.int32), axis=1) - 1
    normed = round_value(rms_norm(x, g_mix))
    projected = tapped(product(normed, w_in), probes[0])
    gate_z = projected[:, :DI]
    conv_in = projected[:, DI : 2 * DI + 2 * NS]
    step_raw = projected[:, 2 * DI + 2 * NS :]
    conv = conv_b[None, :] + conv_w[0][None, :] * conv_in
    for lag in range(1, CONV):
        moved = jnp.concatenate(
            [jnp.zeros((lag, conv_in.shape[1]), conv_in.dtype), conv_in[: count - lag]], 0
        )
        keep_rows = (position >= lag).astype(conv_in.dtype)
        conv = conv + conv_w[lag][None, :] * moved * keep_rows[:, None]
    conv = jax.nn.silu(conv)
    ssm_in = conv[:, :DI].reshape(count, NH, MH).transpose(1, 0, 2)
    b_proj = conv[:, DI : DI + NS]
    c_proj = conv[:, DI + NS :]
    step_size = jax.nn.softplus(step_raw + dt_bias[None, :]).T
    decay_sum = lax.dot_general(
        step_size * (-jnp.exp(a_log))[:, None],
        earlier.astype(jnp.float32),
        (((1,), (1,)), ((), ())),
        precision=lax.Precision.HIGHEST,
    )
    cb_scores = contract("tn,sn->ts", c_proj, b_proj)
    inside = visible[None]
    log_gap = jnp.where(inside, decay_sum[:, :, None] - decay_sum[:, None, :], -1e30)
    mix_weight = jnp.exp(log_gap) * cb_scores[None]
    ssm_out = contract("hts,hsp->htp", mix_weight, ssm_in * step_size[:, :, None])
    ssm_out = ssm_out + d_skip[:, None, None] * ssm_in
    ssm_out = ssm_out.transpose(1, 0, 2).reshape(count, DI) * jax.nn.silu(gate_z)
    gated = round_value(rms_norm(ssm_out, g_ssm))
    mixer = product(gated, w_out)
    qkv = tapped(product(normed, w_qkv), probes[1])
    angle_pos = position.astype(jnp.float32)
    query = rotate(qkv[:, : QH * AH].reshape(count, QH, AH), angle_pos).reshape(
        count, KVH, QH // KVH, AH
    )
    key = rotate(qkv[:, QH * AH : (QH + KVH) * AH].reshape(count, KVH, AH), angle_pos)
    value = qkv[:, (QH + KVH) * AH :].reshape(count, KVH, AH)
    query = round_value(query)
    key = round_value(key)
    value = round_value(value)
    scores = contract("tgqa,sga->gqts", query, key) * AH ** (-0.5)
    scores = jnp.where(visible[None, None], scores, -1e30)
    probs = round_value(jax.nn.softmax(scores, axis=-1))
    context = contract("gqts,sga->tgqa", probs, value).reshape(count, QH * AH)
    context = round_value(context)
    middle = x + tapped(mixer + product(context, w_o), probes[2])
    ffn_in = round_value(rms_norm(middle, g_ffn))
    both = tapped(product(ffn_in, w_gu), probes[3])
    action = round_value(jax.nn.silu(both[:, :FF]) * both[:, FF:])
    result = round_value(middle + product(action, w_down))
    lefts = tuple(v.astype(jnp.bfloat16) for v in (normed, gated, context, ffn_in, action))
    return result, lefts


def partial_layer(docs_here, large):

    def apply_layer(layer_in, small, probes):
        return layer(layer_in, small, probes, docs_here, large)

    return apply_layer


def local(
    tokens,
    cotangent,
    lengths,
    w_in,
    conv_w,
    conv_b,
    dt_bias,
    a_log,
    d_skip,
    g_mix,
    g_ssm,
    w_out,
    w_qkv,
    w_o,
    g_ffn,
    w_gu,
    w_down,
):
    first = lax.axis_index("section") == 0
    large = tuple((w[0] for w in (w_in, w_out, w_qkv, w_o, w_gu, w_down)))
    small = tuple(
        (w[0] for w in (conv_w, conv_b, dt_bias, a_log, d_skip, g_mix, g_ssm, g_ffn))
    )
    widths = (large[0].shape[1], large[2].shape[1], D, 2 * FF)
    probes = tuple((jnp.zeros((MB_TOK, width), jnp.float32) for width in widths))
    inputs = tokens.astype(jnp.float32).reshape(MICRO, MB_TOK, D)
    incoming = cotangent.astype(jnp.float32).reshape(MICRO, MB_TOK, D)
    doc_table = jnp.stack([segments(lengths[0, index]) for index in range(MICRO)])
    received = jnp.zeros((MB_TOK, D), jnp.float32)
    results = []
    backers = []
    lefts = []
    for tick in range(MICRO + 1):
        fresh = inputs[min(tick, MICRO - 1)]
        layer_in = jnp.where(first, fresh, received)
        docs_here = jnp.where(first, doc_table[min(tick, MICRO - 1)], doc_table[max(tick - 1, 0)])
        result, backer, left = jax.vjp(
            partial_layer(docs_here, large), layer_in, small, probes, has_aux=True
        )
        lefts.append(left)
        results.append(result)
        backers.append(backer)
        if tick < MICRO:
            received = passed_along(result.astype(jnp.bfloat16), "section", 1).astype(jnp.float32)
    returned = jnp.zeros((MB_TOK, D), jnp.float32)
    input_grads = [None] * (MICRO + 1)
    local_small = [jnp.zeros_like(w) for w in small]
    rights = [None] * (MICRO + 1)
    for tick in reversed(range(MICRO + 1)):
        if tick >= 1:
            seed_grad = incoming[tick - 1]
        else:
            seed_grad = jnp.zeros((MB_TOK, D), jnp.float32)
        upstream = jnp.where(first, returned, seed_grad)
        grad_raw, grads, taps = backers[tick](upstream)
        rights[tick] = tuple(
            (
                v.astype(jnp.bfloat16)
                for v in (jnp.concatenate([taps[0], taps[1]], 1), taps[2], taps[3], upstream)
            )
        )
        grad_in = round_plain(grad_raw)
        input_grads[tick] = grad_in
        if tick > 0:
            returned = passed_along(grad_in.astype(jnp.bfloat16), "section", -1).astype(jnp.float32)
        local_small = [total + grad for total, grad in zip(local_small, grads)]

    def both_blocks(blocks, which):
        return jnp.concatenate(
            [jnp.where(first, blocks[i][which], blocks[i + 1][which]) for i in range(MICRO)], 0
        )

    def weight_grad(which_left, which_right):
        left = both_blocks(lefts, which_left)
        right = both_blocks(rights, which_right)
        columns = right.shape[1]
        right = jnp.pad(right, ((0, 0), (0, -columns % 128)))
        local_sum = lax.dot_general(
            left, right, (((0,), (0,)), ((), ())), preferred_element_type=jnp.float32
        ).astype(jnp.bfloat16)
        summed = lax.psum_scatter(local_sum, "dp", scatter_dimension=0, tiled=True)
        return summed[:, :columns].astype(jnp.float32)[None]

    grad_w_down = weight_grad(4, 3)
    grad_w_gu = weight_grad(3, 2)
    grad_w_out = weight_grad(1, 1)
    grad_w_o = weight_grad(2, 1)
    grad_w_in_qkv = weight_grad(0, 0)
    grad_w_in = grad_w_in_qkv[:, :, : widths[0]]
    grad_w_qkv = grad_w_in_qkv[:, :, widths[0] :]
    packed = jnp.concatenate([grad.reshape(-1) for grad in local_small])
    packed = lax.psum(packed, "dp")
    summed_small = []
    start = 0
    for weight in small:
        summed_small.append(packed[start : start + weight.size].reshape((1,) + weight.shape))
        start += weight.size

    def own_part(whole):
        part = whole.shape[1] // lax.axis_size("dp")
        return lax.dynamic_slice_in_dim(whole, lax.axis_index("dp") * part, part, 1)

    out_rows = [jnp.where(first, results[index], results[index + 1]) for index in range(MICRO)]
    grad_rows = [
        jnp.where(first, input_grads[index], input_grads[index + 1]) for index in range(MICRO)
    ]
    layer_out = jnp.concatenate(out_rows, 0)[None].astype(jnp.bfloat16)
    input_grad = jnp.concatenate(grad_rows, 0)[None].astype(jnp.bfloat16)
    grad_conv_w, grad_conv_b, grad_dt_bias, grad_a_log, grad_d_skip = summed_small[:5]
    grad_g_mix, grad_g_ssm, grad_g_ffn = (own_part(whole) for whole in summed_small[5:])
    return (
        layer_out,
        input_grad,
        grad_w_in,
        grad_conv_w,
        grad_conv_b,
        grad_dt_bias,
        grad_a_log,
        grad_d_skip,
        grad_g_mix,
        grad_g_ssm,
        grad_w_out,
        grad_w_qkv,
        grad_w_o,
        grad_g_ffn,
        grad_w_gu,
        grad_w_down,
    )


def solution(mesh):
    in_specs = (
        P("dp", None),
        P("dp", None),
        P("dp", None, None),
        P("section", None, None),
        P("section", None, None),
        P("section", None),
        P("section", None),
        P("section", None),
        P("section", None),
        P("section", None),
        P("section", None),
        P("section", None, None),
        P("section", None, None),
        P("section", None, None),
        P("section", None),
        P("section", None, None),
        P("section", None, None),
    )
    out_specs = (
        P("section", "dp", None),
        P("section", "dp", None),
        P("section", "dp", None),
        P("section", None, None),
        P("section", None),
        P("section", None),
        P("section", None),
        P("section", None),
        P("section", "dp"),
        P("section", "dp"),
        P("section", "dp", None),
        P("section", "dp", None),
        P("section", "dp", None),
        P("section", "dp"),
        P("section", "dp", None),
        P("section", "dp", None),
    )
    return jax.shard_map(local, mesh=mesh, in_specs=in_specs, out_specs=out_specs, check_vma=False)
```
